32 devices in a mesh: sq: 32 (over z, y, x, core).
Axes of the slice: x: 2, y: 2, z: 4, core: 2. Of those that a mesh axis runs over, the one named last changes fastest.
Arguments:
- tokens: bfloat16 [1024, 2880], P('sq'), may hold values from -6 to 6
- norm_gain: float32 [2880], replicated, may hold values from 0.25 to 1.75
- expert_ids: int32 [1024, 4], P('sq'), may hold values from 0 to 7, all different within a row; in each aligned block of 32 rows (0 to 31, 32 to 63, ...) at most 17 rows name the same one
- combine_weight: float32 [1024, 4], P('sq'), may hold values from 0.05 to 0.6
- cotangent: bfloat16 [1024, 2880], P('sq'), may hold values from -6 to 6
- w_gate: bfloat16 [32, 2880, 720], P('sq'), may hold values from -0.109375 to 0.109375
- w_up: bfloat16 [32, 2880, 720], P('sq'), may hold values from -0.109375 to 0.109375
- w_down: bfloat16 [32, 720, 2880], P('sq'), may hold values from -0.109375 to 0.109375
Outputs:
- d_tokens: bfloat16 [1024, 2880], P('sq')
- grad_gate: bfloat16 [32, 2880, 720], P('sq')
- grad_up: bfloat16 [32, 2880, 720], P('sq')
- grad_down: bfloat16 [32, 720, 2880], P('sq')
The draws below stay inside these ranges and needn't reach their ends.
Inputs may be any that keep to these rules, and one draw needn't show every extreme that they name: `expert_ids`: each row names 4 different experts; the rows of one device name any one expert at most 17 times, a bound that some block reaches.
All inputs are finite; a program needn't handle non-finite values.
Results may differ from the reference program's by a relative error of at most 0.0078.
Values may be sent and summed in bfloat16 or wider, within the bound.
No kernel may reach another device: no remote copies, remote signals or barrier semaphores. Data moves between devices by JAX's collectives and lax.ppermute only.
A program may use at most 128 MiB of HBM per device.

```python
import math
import jax
import jax.numpy as jnp
import numpy as np
from jax import lax

D = 2880
FF = 2880
TOP = 4
QUARTERS = 4
TOK_DEV = 32
TOKENS = 1024
EXPERTS = 8
FF_Q = 720
SLOTS = 17
N_SQ = 32


def block_scale(stream_key, shape, pieces, least, top_value):
    level, own = 1.0, jax.random.fold_in(stream_key, 6)
    for dim, blocks in pieces:
        steps = jnp.exp(jax.random.uniform(jax.random.fold_in(own, dim), (blocks,), jnp.float32, least / len(pieces), top_value / len(pieces)))
        level = level * jnp.repeat(steps, shape[dim] // blocks).reshape([-1 if axis == dim else 1 for axis in range(len(shape))])
    return level


def routed_block(stream_key, own, number, rows, amount, top, bound, slope):
    sequence = jax.random.permutation(stream_key, amount)
    heavy_load, common = portions_of(amount, rows * top, bound, slope, True), portions_of(amount, rows * top, bound, slope, False)
    places = jnp.arange(amount)

    def named(lengths, offset_by):
        used = int((lengths > 0).sum())
        fixed = max(1, used // 4)
        moved = fixed + (places - fixed + offset_by * (used - fixed)) % max(1, amount - fixed)
        return jnp.zeros((amount,), jnp.int32).at[sequence[jnp.where(places < fixed, places, moved)]].set(jnp.asarray(lengths, jnp.int32))

    lengths = jnp.where(number % 4 == 0, named(heavy_load, number // 4), named(common, number - number // 4 - 1))
    mixed = jax.random.permutation(jax.random.fold_in(own, 3), amount)
    giver, receiver = mixed[0:amount // 2 * 2:2], mixed[1:amount // 2 * 2:2]
    slack = jnp.minimum(lengths[giver] - 1, bound - lengths[receiver]) // 2
    slack = jnp.where((giver == sequence[0]) | (receiver == sequence[0]) | (lengths[receiver] == 0), 0, jnp.maximum(slack, 0))
    moved = jax.random.randint(jax.random.fold_in(own, 4), (amount // 2,), 0, 1 << 20) % (slack + 1)
    lengths = lengths.at[giver].add(-moved).at[receiver].add(moved)
    items = jnp.searchsorted(jnp.cumsum(lengths), jnp.arange(rows * top), side="right").astype(jnp.int32)
    grid = items.reshape(top, rows).T
    grid = grid[jax.random.permutation(jax.random.fold_in(own, 1), rows)]
    offset_by = jax.random.randint(jax.random.fold_in(own, 2), (rows, 1), 0, top)
    return jnp.take_along_axis(grid, (jnp.arange(top)[None, :] + offset_by) % top, axis=1)


def portions_of(number_of, total, bound, lean, full):
    loads = [(1 << 20) // math.isqrt(rank ** lean) + 1 for rank in range(1, number_of + 1)]
    largest = bound if full else min(bound, max(-(-total // number_of), total * loads[0] // sum(loads)))
    least = 1 if total - largest >= number_of - 1 else 0
    holding, surplus = [largest] + [least] * (number_of - 1), total - largest - least * (number_of - 1)
    while surplus > 0:
        free = [i for i in range(1, number_of) if holding[i] < largest] or [i for i in range(1, number_of) if holding[i] < bound]
        pool, left = sum([loads[i] for i in free]), surplus
        for i in free:
            addition = min(bound - holding[i], max(1, left * loads[i] // pool), surplus)
            holding[i] = holding[i] + addition
            surplus = surplus - addition
    return np.array(holding)


def scatter_about(rng, extent, scale, reach, cuts=(), kind=jnp.bfloat16):
    values = jax.random.normal(rng, extent, jnp.float32) * scale
    if len(cuts) > 0:
        values = block_scale(rng, extent, cuts, -0.22, 0.18) * values
    return jnp.clip(values, min=-reach, max=reach).astype(kind)


def setup_inputs(seed: int = 0) -> dict:
    arg_keys = jax.random.split(jax.random.key(seed), 9)
    tokens = scatter_about(arg_keys[0], (TOKENS, D), 1.0, 6.0, ((0, 32),))
    norm_gain = jnp.clip(1.0 + 0.15 * jax.random.normal(arg_keys[1], (D,), jnp.float32), 0.25, 1.75)
    expert_ids_keys = jax.random.split(jax.random.fold_in(arg_keys[2], 1), TOKENS // TOK_DEV)
    expert_ids_turns = jax.random.permutation(jax.random.fold_in(arg_keys[2], 3), TOKENS // TOK_DEV)
    expert_ids = jax.vmap(lambda own, number: routed_block(jax.random.fold_in(arg_keys[2], 2), own, number, TOK_DEV, EXPERTS, TOP, SLOTS, 2))(expert_ids_keys, expert_ids_turns).reshape((TOKENS, TOP))
    combine_weight = jnp.clip(jnp.exp(math.log(0.6) - 2.4849067 * jax.random.uniform(arg_keys[3], (TOKENS, TOP), jnp.float32) ** block_scale(arg_keys[3], (TOKENS, TOP), ((0, 32),), -0.2, 0.2)), 0.05, 0.6)
    cotangent = scatter_about(arg_keys[4], (TOKENS, D), 1.0, 6.0, ((0, 32),))
    w_gate = scatter_about(arg_keys[5], (EXPERTS * QUARTERS, D, FF_Q), D ** -0.5, 0.109375, ((0, 32),))
    w_up = scatter_about(arg_keys[6], (EXPERTS * QUARTERS, D, FF_Q), D ** -0.5, 0.109375, ((0, 32),))
    w_down = scatter_about(arg_keys[7], (EXPERTS * QUARTERS, FF_Q, D), FF ** -0.5, 0.109375, ((0, 32),))
    return {"tokens": tokens, "norm_gain": norm_gain, "expert_ids": expert_ids, "combine_weight": combine_weight, "cotangent": cotangent, "w_gate": w_gate, "w_up": w_up, "w_down": w_down}


norm_eps = 1e-05
glu_alpha = 1.702

def expert_backward(x_in, dy_e, gate_w, up_w, down_w):
    gate = jnp.dot(x_in, gate_w, preferred_element_type=jnp.float32)
    up = jnp.dot(x_in, up_w, preferred_element_type=jnp.float32)
    sig = jax.nn.sigmoid(glu_alpha * gate)
    glu = gate * sig
    hid = (glu * (up + 1.0)).astype(jnp.bfloat16)
    d_hid = jnp.dot(dy_e, down_w.T, preferred_element_type=jnp.float32)
    d_up = (d_hid * glu).astype(jnp.bfloat16)
    d_gate = (d_hid * (up + 1.0) * (sig + glu_alpha * gate * sig * (1.0 - sig))).astype(jnp.bfloat16)
    partial_rows = jnp.dot(d_gate, gate_w.T, preferred_element_type=jnp.float32) + jnp.dot(d_up, up_w.T, preferred_element_type=jnp.float32)
    grad_g = jnp.dot(x_in.T, d_gate, preferred_element_type=jnp.float32).astype(jnp.bfloat16)
    grad_u = jnp.dot(x_in.T, d_up, preferred_element_type=jnp.float32).astype(jnp.bfloat16)
    grad_d = jnp.dot(hid.T, dy_e, preferred_element_type=jnp.float32).astype(jnp.bfloat16)
    return (partial_rows.astype(jnp.bfloat16), grad_g, grad_u, grad_d)

def reference(tokens, norm_gain, expert_ids, combine_weight, cotangent, w_gate, w_up, w_down):
    token_f = tokens.astype(jnp.float32)
    rstd = lax.rsqrt(lax.optimization_barrier(jnp.mean(token_f * token_f, axis=-1, keepdims=True)) + norm_eps)
    normed = (token_f * rstd * norm_gain).astype(jnp.bfloat16)
    picks = expert_ids.reshape(N_SQ, TOK_DEV * TOP)
    onehot = (picks[:, :, None] == jnp.arange(EXPERTS, dtype=jnp.int32)[None, None, :]).astype(jnp.int32)
    earlier = jnp.cumsum(onehot, axis=1) - onehot
    slot = lax.optimization_barrier(jnp.sum(earlier * onehot, axis=-1)).astype(jnp.int32)
    source = jnp.arange(N_SQ, dtype=jnp.int32)[:, None]
    position = (source * SLOTS + slot).reshape(-1).astype(jnp.int32)
    flat_expert = expert_ids.reshape(-1).astype(jnp.int32)
    pick_index = jnp.arange(TOKENS * TOP, dtype=jnp.int32)
    table = jnp.zeros((EXPERTS, N_SQ * SLOTS), jnp.int32).at[flat_expert, position].set(pick_index + 1)
    dy_pick = (combine_weight.reshape(-1)[:, None] * cotangent.astype(jnp.float32)[pick_index // TOP]).astype(jnp.bfloat16)

    def per_expert(inputs):
        entry, gate4, up4, down4 = inputs
        valid = (entry > 0)[:, None]
        which = jnp.maximum(entry - 1, 0).astype(jnp.int32)
        x_in = jnp.where(valid, normed[which // TOP], jnp.zeros((), jnp.bfloat16))
        dy_e = jnp.where(valid, dy_pick[which], jnp.zeros((), jnp.bfloat16))
        total = jnp.zeros((N_SQ * SLOTS, D), jnp.float32)
        grads_g, grads_u, grads_d = ([], [], [])
        for quarter in range(QUARTERS):
            part, grad_g, grad_u, grad_d = expert_backward(x_in, dy_e, gate4[quarter], up4[quarter], down4[quarter])
            total = total + part.astype(jnp.float32)
            grads_g.append(grad_g)
            grads_u.append(grad_u)
            grads_d.append(grad_d)
        return (total.astype(jnp.bfloat16), jnp.stack(grads_g), jnp.stack(grads_u), jnp.stack(grads_d))
    d_rows, grad_gate, grad_up, grad_down = lax.map(per_expert, (table, w_gate.reshape(EXPERTS, QUARTERS, D, FF_Q), w_up.reshape(EXPERTS, QUARTERS, D, FF_Q), w_down.reshape(EXPERTS, QUARTERS, FF_Q, D)))
    d_pick = d_rows[flat_expert, position].astype(jnp.float32)
    d_normed = lax.optimization_barrier(jnp.sum(d_pick.reshape(TOKENS, TOP, D), axis=1))
    scaled = d_normed * norm_gain
    mixed = lax.optimization_barrier(jnp.mean(token_f * scaled, axis=-1, keepdims=True))
    d_tokens = (rstd * scaled - token_f * rstd * rstd * rstd * mixed).astype(jnp.bfloat16)
    return (d_tokens, grad_gate.reshape(EXPERTS * QUARTERS, D, FF_Q), grad_up.reshape(EXPERTS * QUARTERS, D, FF_Q), grad_down.reshape(EXPERTS * QUARTERS, FF_Q, D))
```

```python
import jax
import jax.numpy as jnp
from jax import lax
from jax.experimental.layout import Layout, with_layout_constraint
from jax.sharding import PartitionSpec as P

QUARTERS = 4
CORE, PAIR, SIDE = 1, 2, 4
TILE = 8

norm_eps = 1e-05
glu_alpha = 1.702


def contract_rows(left, right):
    return lax.dot_general(
        left, right, (((0,), (0,)), ((), ())), preferred_element_type=jnp.float32
    )


def contract_cols(left, right):
    return lax.dot_general(
        left, right, (((1,), (1,)), ((), ())), preferred_element_type=jnp.float32
    )


def row_major(value):
    return with_layout_constraint(value, Layout(major_to_minor=(0, 1)))


def behind(values, first):
    return lax.optimization_barrier((values, first))[0]


def three_parts(value):
    first = lax.reduce_precision(value, 8, 7)
    rest = value - first
    second = lax.reduce_precision(rest, 8, 7)
    return [part.astype(jnp.bfloat16) for part in (first, second, rest - second)]


def local(tokens, norm_gain, expert_ids, combine_weight, cotangent, w_gate, w_up, w_down):
    devices = lax.axis_size("sq")
    tok_count, top_count = expert_ids.shape
    width = tokens.shape[1]
    expert_count = devices // QUARTERS
    planes = expert_count // 2
    slot_count = tok_count * top_count * QUARTERS // devices + 1
    slots = -(-slot_count * planes // TILE) * TILE
    column = planes * tok_count
    kept = 2 * slots
    expert = lax.axis_index("sq") // QUARTERS
    plane = expert // 2

    def flip(value, bit):
        return lax.ppermute(row_major(value), "sq", [(i, i ^ bit) for i in range(devices)])

    def shift(value, by):
        step = by * 2 * QUARTERS
        pairs = [(i, (i + step) % devices) for i in range(devices)]
        return lax.ppermute(row_major(value), "sq", pairs)

    token_f = row_major(tokens).astype(jnp.float32)
    rstd = lax.rsqrt(jnp.mean(token_f * token_f, axis=-1, keepdims=True) + norm_eps)
    normed = (token_f * rstd * norm_gain).astype(jnp.bfloat16)

    picked = expert_ids[:, :, None] == jnp.arange(expert_count, dtype=jnp.int32)[None, None, :]
    weight = jnp.sum(jnp.where(picked, combine_weight[:, :, None], 0.0), axis=1)
    payload = row_major(jnp.concatenate([normed] + three_parts(weight), axis=1))

    lines = [
        [plane * 2 * QUARTERS + place for plane in range(planes)] for place in range(2 * QUARTERS)
    ]

    def gather_column(block):
        return row_major(
            lax.all_gather(block, "sq", axis=0, tiled=True, axis_index_groups=lines)
        )

    column_x = gather_column(payload)

    parts = column_x[:, width:].astype(jnp.float32).reshape(column, 3, expert_count)
    column_weight = parts[:, 0] + parts[:, 1] + parts[:, 2]
    slot_iota = lax.broadcasted_iota(jnp.int32, (slots, column), 0)
    earlier = lax.broadcasted_iota(jnp.int32, (column, column), 0) < lax.broadcasted_iota(
        jnp.int32, (column, column), 1
    )

    def choose(which):
        experts = jnp.arange(expert_count, dtype=jnp.int32)
        mine = jnp.sum(jnp.where(experts[None, :] == which, column_weight, 0.0), axis=1)
        mask = mine > 0.0
        slot = jnp.sum(jnp.where(earlier & mask[:, None], 1, 0), axis=0)
        hit = (slot_iota == slot[None, :]) & mask[None, :]
        row_weight = jnp.sum(jnp.where(hit, mine[None, :], 0.0), axis=1, keepdims=True)
        return hit.astype(jnp.bfloat16), row_weight

    own_select, own_weight = choose(expert)
    far_select, far_weight = choose(expert ^ 1)

    def rows_x(select):
        return jnp.dot(select, column_x[:, :width], preferred_element_type=jnp.float32).astype(
            jnp.bfloat16
        )

    own_x = rows_x(own_select)
    far_x = rows_x(far_select)
    side_x = flip(far_x, SIDE)
    pair_x = flip(own_x, PAIR)
    across_x = flip(far_x, PAIR | SIDE)
    column_cot = behind(gather_column(cotangent), (side_x, pair_x, across_x))

    def rows_dy(select, row_weight):
        rows = jnp.dot(select, column_cot, preferred_element_type=jnp.float32)
        return (rows * row_weight).astype(jnp.bfloat16)

    own_dy = rows_dy(own_select, own_weight)
    far_dy = rows_dy(far_select, far_weight)
    side_dy = flip(far_dy, SIDE)
    pair_dy = flip(own_dy, PAIR)

    def both_cores(first, second):
        rows = jnp.concatenate([first, second], axis=0)
        return jnp.concatenate([rows, flip(rows, CORE)], axis=0)

    gate_w = w_gate[0]
    up_w = w_up[0]
    down_w = w_down[0]

    def forward(x_in):
        gate = jnp.dot(x_in, gate_w, preferred_element_type=jnp.float32)
        up = jnp.dot(x_in, up_w, preferred_element_type=jnp.float32)
        return gate, up

    def hidden(gate, up, dy_e):
        sig = jax.nn.sigmoid(glu_alpha * gate)
        glu = gate * sig
        hid = (glu * (up + 1.0)).astype(jnp.bfloat16)
        d_hid = contract_cols(dy_e, down_w)
        d_up = (d_hid * glu).astype(jnp.bfloat16)
        d_gate = (d_hid * (up + 1.0) * (sig + glu_alpha * gate * sig * (1.0 - sig))).astype(
            jnp.bfloat16
        )
        return hid, d_gate, d_up

    def row_gradient(d_gate, d_up, first, last):
        return (
            contract_cols(d_gate, gate_w[first:last]) + contract_cols(d_up, up_w[first:last])
        ).astype(jnp.bfloat16)

    own_x, side_x, pair_x, across_x = behind((own_x, side_x, pair_x, across_x), (own_dy, far_dy))
    chip_x = both_cores(own_x, side_x)
    pair_x = both_cores(pair_x, across_x)
    chip_forward = forward(chip_x)
    side_dy, pair_dy = behind((side_dy, pair_dy), chip_forward)
    across_dy = flip(side_dy, PAIR)
    chip_dy = both_cores(own_dy, side_dy)
    pair_forward = forward(behind(pair_x, chip_dy))
    chip_hid, chip_d_gate, chip_d_up = hidden(*chip_forward, chip_dy)
    chip_rows = row_gradient(chip_d_gate, chip_d_up, 0, width)
    chip_sum = chip_rows[:kept].astype(jnp.float32) + flip(chip_rows[kept:], CORE).astype(
        jnp.float32
    )
    side_sum = flip(chip_sum[slots:].astype(jnp.bfloat16), SIDE)

    pair_core_dy = flip(pair_dy, CORE)
    across_dy = behind(across_dy, (chip_sum, pair_forward))
    pair_dy = jnp.concatenate([pair_dy, across_dy, pair_core_dy, flip(across_dy, CORE)], axis=0)
    pair_hid, pair_d_gate, pair_d_up = hidden(*pair_forward, pair_dy)

    cut = -(-width // 2 // 256) * 256
    spans = [(0, cut), (cut, width)]

    def core_sum(rows, from_core):
        total = rows[:kept].astype(jnp.float32) + from_core.astype(jnp.float32)
        return total.astype(jnp.bfloat16)

    def to_pair(rows):
        return flip(rows[:slots], PAIR), flip(rows[slots:], PAIR | SIDE)

    rows_first = row_gradient(pair_d_gate, pair_d_up, *spans[0])
    core_first = flip(rows_first[kept:], CORE)
    rows_second = row_gradient(*behind((pair_d_gate, pair_d_up), rows_first), *spans[1])
    core_second = flip(rows_second[kept:], CORE)
    sum_first = core_sum(rows_first, core_first)
    sent_first = to_pair(sum_first)

    x_in = jnp.concatenate([chip_x, pair_x], axis=0)
    dy_e = jnp.concatenate([chip_dy, pair_dy], axis=0)
    hid = jnp.concatenate([chip_hid, pair_hid], axis=0)
    d_gate = jnp.concatenate([chip_d_gate, pair_d_gate], axis=0)
    d_up = jnp.concatenate([chip_d_up, pair_d_up], axis=0)

    def to_column(span, from_pair, from_across):
        first, last = span
        own_rows = chip_sum[:slots, first:last] + from_pair.astype(jnp.float32)
        far_rows = side_sum[:, first:last].astype(jnp.float32) + from_across.astype(jnp.float32)
        return row_major(
            contract_rows(own_select, own_rows.astype(jnp.bfloat16))
            + contract_rows(far_select, far_rows.astype(jnp.bfloat16))
        )

    def to_tokens(d_column):
        blocks = d_column.reshape(planes, tok_count, d_column.shape[1])
        total = lax.dynamic_index_in_dim(blocks, plane, 0, False)
        got = []
        for s in range(1, planes):
            block = lax.dynamic_index_in_dim(blocks, (plane + s) % planes, 0, False)
            got.append(shift(block.astype(jnp.bfloat16), s))
        return total, got

    def added(total, got):
        for block in got:
            total = total + block.astype(jnp.float32)
        return total

    def weight_gradient(left, right, first):
        return contract_rows(*behind((left, right), first)).astype(jnp.bfloat16)

    sum_second = core_sum(*behind((rows_second, core_second), sum_first))
    sent_second = to_pair(sum_second)
    grad_gate = weight_gradient(x_in, d_gate, (sum_second, chip_sum))
    d_column = to_column(spans[0], *behind(sent_first, grad_gate))
    first_half = to_tokens(d_column)
    grad_up = weight_gradient(x_in, d_up, d_column)
    first_half = added(*behind(first_half, grad_up))
    second_half = to_tokens(to_column(spans[1], *behind(sent_second, first_half)))
    grad_down = weight_gradient(hid, dy_e, first_half)
    second_half = added(*behind(second_half, grad_down))
    grads = [grad[None] for grad in (grad_gate, grad_up, grad_down)]
    d_normed = jnp.concatenate([first_half, second_half], axis=1)

    scaled = d_normed * norm_gain
    mixed = jnp.mean(token_f * scaled, axis=-1, keepdims=True)
    d_tokens = (rstd * scaled - token_f * rstd * rstd * rstd * mixed).astype(jnp.bfloat16)
    return (d_tokens, *grads)


def solution(mesh):
    placed = (
        P("sq", None),
        P(),
        P("sq", None),
        P("sq", None),
        P("sq", None),
        P("sq", None, None),
        P("sq", None, None),
        P("sq", None, None),
    )
    return jax.shard_map(
        local,
        mesh=mesh,
        in_specs=placed,
        out_specs=(P("sq", None), P("sq", None, None), P("sq", None, None), P("sq", None, None)),
        check_vma=False,
    )
```

```python
import jax
import jax.numpy as jnp
from jax import lax
from jax.experimental import pallas as pl
from jax.experimental.layout import Layout, with_layout_constraint
from jax.experimental.pallas import tpu as pltpu
from jax.sharding import PartitionSpec as P

QUARTERS = 4
CORE, PAIR, SIDE = 1, 2, 4
TILE = 8
PRODUCT_COLUMNS = 768

norm_eps = 1e-05
glu_alpha = 1.702


def contract_rows(left, right):
    return lax.dot_general(
        left, right, (((0,), (0,)), ((), ())), preferred_element_type=jnp.float32
    )


def contract_cols(left, right):
    return lax.dot_general(
        left, right, (((1,), (1,)), ((), ())), preferred_element_type=jnp.float32
    )


def row_major(value):
    return with_layout_constraint(value, Layout(major_to_minor=(0, 1)))


def behind(values, first):
    return lax.optimization_barrier((values, first))[0]


def fast_copy_kernel(weight_ref, out_ref, done):
    copy = pltpu.make_async_copy(weight_ref, out_ref, done)
    copy.start()
    copy.wait()


def fast_copy(weight):
    return pl.pallas_call(
        fast_copy_kernel,
        in_specs=[pl.BlockSpec(memory_space=pl.ANY)],
        out_specs=pl.BlockSpec(memory_space=pltpu.VMEM),
        out_shape=jax.ShapeDtypeStruct(weight.shape, weight.dtype),
        scratch_shapes=[pltpu.SemaphoreType.DMA],
        cost_estimate=pl.CostEstimate(
            flops=0, bytes_accessed=4 * weight.size, transcendentals=0
        ),
        compiler_params=pltpu.CompilerParams(vmem_limit_bytes=8 * 1024 * 1024),
    )(weight)


def product_kernel(left_ref, right_ref, out_ref, turned_ref, result_ref, sent):
    turned_ref[...] = left_ref[...].T
    width = right_ref.shape[1]
    copies = []
    for number, first in enumerate(range(0, width, PRODUCT_COLUMNS)):
        columns = slice(first, min(first + PRODUCT_COLUMNS, width))
        result_ref[:, columns] = jnp.dot(
            turned_ref[...], right_ref[:, columns], preferred_element_type=jnp.float32
        ).astype(result_ref.dtype)
        copies.append(
            pltpu.make_async_copy(
                result_ref.at[:, columns], out_ref.at[:, columns], sent.at[number]
            )
        )
        copies[-1].start()
    for copy in copies:
        copy.wait()


def weight_product(left, right):
    rows, hidden = left.shape
    width = right.shape[1]
    return pl.pallas_call(
        product_kernel,
        in_specs=[pl.BlockSpec(memory_space=pltpu.VMEM)] * 2,
        out_specs=pl.BlockSpec(memory_space=pl.ANY),
        out_shape=jax.ShapeDtypeStruct((hidden, width), jnp.bfloat16),
        scratch_shapes=[
            pltpu.VMEM((hidden, rows), jnp.bfloat16),
            pltpu.VMEM((hidden, width), jnp.bfloat16),
            pltpu.SemaphoreType.DMA((-(-width // PRODUCT_COLUMNS),)),
        ],
        cost_estimate=pl.CostEstimate(
            flops=2 * rows * hidden * width,
            bytes_accessed=2 * (rows * hidden + rows * width + hidden * width),
            transcendentals=0,
        ),
        compiler_params=pltpu.CompilerParams(vmem_limit_bytes=24 * 1024 * 1024),
    )(left, right)


def three_parts(value):
    first = lax.reduce_precision(value, 8, 7)
    rest = value - first
    second = lax.reduce_precision(rest, 8, 7)
    return [part.astype(jnp.bfloat16) for part in (first, second, rest - second)]


def local(tokens, norm_gain, expert_ids, combine_weight, cotangent, w_gate, w_up, w_down):
    devices = lax.axis_size("sq")
    tok_count, top_count = expert_ids.shape
    width = tokens.shape[1]
    expert_count = devices // QUARTERS
    planes = expert_count // 2
    slot_count = tok_count * top_count * QUARTERS // devices + 1
    slots = -(-slot_count * planes // TILE) * TILE
    column = planes * tok_count
    kept = 2 * slots
    expert = lax.axis_index("sq") // QUARTERS
    plane = expert // 2

    def flip(value, bit):
        return lax.ppermute(row_major(value), "sq", [(i, i ^ bit) for i in range(devices)])

    def shift(value, by):
        step = by * 2 * QUARTERS
        pairs = [(i, (i + step) % devices) for i in range(devices)]
        return lax.ppermute(row_major(value), "sq", pairs)

    token_f = row_major(tokens).astype(jnp.float32)
    rstd = lax.rsqrt(jnp.mean(token_f * token_f, axis=-1, keepdims=True) + norm_eps)
    normed = (token_f * rstd * norm_gain).astype(jnp.bfloat16)

    picked = expert_ids[:, :, None] == jnp.arange(expert_count, dtype=jnp.int32)[None, None, :]
    weight = jnp.sum(jnp.where(picked, combine_weight[:, :, None], 0.0), axis=1)
    payload = row_major(jnp.concatenate([normed] + three_parts(weight), axis=1))

    lines = [
        [plane * 2 * QUARTERS + place for plane in range(planes)] for place in range(2 * QUARTERS)
    ]

    def gather_column(block):
        return row_major(
            lax.all_gather(block, "sq", axis=0, tiled=True, axis_index_groups=lines)
        )

    column_x = gather_column(payload)

    parts = column_x[:, width:].astype(jnp.float32).reshape(column, 3, expert_count)
    column_weight = parts[:, 0] + parts[:, 1] + parts[:, 2]
    slot_iota = lax.broadcasted_iota(jnp.int32, (slots, column), 0)
    earlier = lax.broadcasted_iota(jnp.int32, (column, column), 0) < lax.broadcasted_iota(
        jnp.int32, (column, column), 1
    )

    def choose(which):
        experts = jnp.arange(expert_count, dtype=jnp.int32)
        mine = jnp.sum(jnp.where(experts[None, :] == which, column_weight, 0.0), axis=1)
        mask = mine > 0.0
        slot = jnp.sum(jnp.where(earlier & mask[:, None], 1, 0), axis=0)
        hit = (slot_iota == slot[None, :]) & mask[None, :]
        row_weight = jnp.sum(jnp.where(hit, mine[None, :], 0.0), axis=1, keepdims=True)
        return hit.astype(jnp.bfloat16), row_weight

    own_select, own_weight = choose(expert)
    far_select, far_weight = choose(expert ^ 1)

    def rows_x(select):
        return jnp.dot(select, column_x[:, :width], preferred_element_type=jnp.float32).astype(
            jnp.bfloat16
        )

    own_x = rows_x(own_select)
    far_x = rows_x(far_select)
    side_x = flip(far_x, SIDE)
    pair_x = flip(own_x, PAIR)
    across_x = flip(far_x, PAIR | SIDE)
    column_cot = behind(gather_column(cotangent), (side_x, pair_x, across_x))

    def rows_dy(select, row_weight):
        rows = jnp.dot(select, column_cot, preferred_element_type=jnp.float32)
        return (rows * row_weight).astype(jnp.bfloat16)

    own_dy = rows_dy(own_select, own_weight)
    far_dy = rows_dy(far_select, far_weight)
    side_dy = flip(far_dy, SIDE)
    pair_dy = flip(own_dy, PAIR)

    def both_cores(first, second):
        rows = jnp.concatenate([first, second], axis=0)
        return jnp.concatenate([rows, flip(rows, CORE)], axis=0)

    gate_w = fast_copy(behind(w_gate[0], (own_dy, far_dy)).T).T
    up_w = w_up[0]
    down_w = fast_copy(behind(w_down[0], gate_w))

    def forward(x_in):
        gate = jnp.dot(x_in, gate_w, preferred_element_type=jnp.float32)
        up = jnp.dot(x_in, up_w, preferred_element_type=jnp.float32)
        return gate, up

    def hidden(gate, up, dy_e):
        sig = jax.nn.sigmoid(glu_alpha * gate)
        glu = gate * sig
        hid = (glu * (up + 1.0)).astype(jnp.bfloat16)
        d_hid = contract_cols(dy_e, down_w)
        d_up = (d_hid * glu).astype(jnp.bfloat16)
        d_gate = (d_hid * (up + 1.0) * (sig + glu_alpha * gate * sig * (1.0 - sig))).astype(
            jnp.bfloat16
        )
        return hid, d_gate, d_up

    def row_gradient(d_gate, d_up, first, last):
        return (
            contract_cols(d_gate, gate_w[first:last]) + contract_cols(d_up, up_w[first:last])
        ).astype(jnp.bfloat16)

    own_x, side_x, pair_x, across_x = behind((own_x, side_x, pair_x, across_x), (own_dy, far_dy))
    chip_x = both_cores(own_x, side_x)
    pair_x = both_cores(pair_x, across_x)
    chip_forward = forward(chip_x)
    side_dy, pair_dy = behind((side_dy, pair_dy), chip_forward)
    across_dy = flip(side_dy, PAIR)
    chip_dy = both_cores(own_dy, side_dy)
    pair_forward = forward(behind(pair_x, chip_dy))
    chip_hid, chip_d_gate, chip_d_up = hidden(*chip_forward, chip_dy)
    chip_rows = row_gradient(chip_d_gate, chip_d_up, 0, width)
    chip_sum = chip_rows[:kept].astype(jnp.float32) + flip(chip_rows[kept:], CORE).astype(
        jnp.float32
    )
    side_sum = flip(chip_sum[slots:].astype(jnp.bfloat16), SIDE)

    pair_core_dy = flip(pair_dy, CORE)
    across_dy = behind(across_dy, (chip_rows, pair_forward))
    pair_dy = jnp.concatenate([pair_dy, across_dy, pair_core_dy, flip(across_dy, CORE)], axis=0)
    pair_hid, pair_d_gate, pair_d_up = hidden(*pair_forward, pair_dy)

    cut = -(-width // 2 // 256) * 256
    spans = [(0, cut), (cut, width)]

    def core_sum(rows, from_core):
        total = rows[:kept].astype(jnp.float32) + from_core.astype(jnp.float32)
        return total.astype(jnp.bfloat16)

    def to_pair(rows):
        return flip(rows[:slots], PAIR), flip(rows[slots:], PAIR | SIDE)

    rows_first = row_gradient(*behind((pair_d_gate, pair_d_up), chip_sum), *spans[0])
    core_first = flip(rows_first[kept:], CORE)
    rows_second = row_gradient(*behind((pair_d_gate, pair_d_up), rows_first), *spans[1])
    core_second = flip(rows_second[kept:], CORE)
    sum_first = core_sum(rows_first, core_first)
    sent_first = to_pair(sum_first)

    x_in = jnp.concatenate([chip_x, pair_x], axis=0)
    dy_e = jnp.concatenate([chip_dy, pair_dy], axis=0)
    hid = jnp.concatenate([chip_hid, pair_hid], axis=0)
    d_gate = jnp.concatenate([chip_d_gate, pair_d_gate], axis=0)
    d_up = jnp.concatenate([chip_d_up, pair_d_up], axis=0)

    def to_column(span, from_pair, from_across):
        first, last = span
        own_rows = chip_sum[:slots, first:last] + from_pair.astype(jnp.float32)
        far_rows = side_sum[:, first:last].astype(jnp.float32) + from_across.astype(jnp.float32)
        return row_major(
            contract_rows(own_select, own_rows.astype(jnp.bfloat16))
            + contract_rows(far_select, far_rows.astype(jnp.bfloat16))
        )

    def to_tokens(d_column):
        blocks = d_column.reshape(planes, tok_count, d_column.shape[1])
        total = lax.dynamic_index_in_dim(blocks, plane, 0, False)
        got = []
        for s in range(1, planes):
            block = lax.dynamic_index_in_dim(blocks, (plane + s) % planes, 0, False)
            got.append(shift(block.astype(jnp.bfloat16), s))
        return total, got

    def added(total, got):
        for block in got:
            total = total + block.astype(jnp.float32)
        return total

    def weight_gradient(hidden_rows, model_rows, first):
        return weight_product(*behind((hidden_rows, model_rows), first))

    grad_gate = weight_gradient(d_gate, x_in, (sum_first, rows_second, chip_sum))
    sum_second = core_sum(*behind((rows_second, core_second), grad_gate))
    sent_second = to_pair(sum_second)
    d_column = to_column(spans[0], *behind(sent_first, grad_gate))
    first_half = to_tokens(d_column)
    grad_up = weight_gradient(d_up, x_in, d_column)
    first_half = added(*behind(first_half, grad_up))
    second_half = to_tokens(to_column(spans[1], *behind(sent_second, first_half)))
    grad_down = weight_gradient(hid, dy_e, first_half)
    second_half = added(*behind(second_half, grad_down))
    grads = [grad_gate.T[None], grad_up.T[None], grad_down[None]]
    d_normed = jnp.concatenate([first_half, second_half], axis=1)

    scaled = d_normed * norm_gain
    mixed = jnp.mean(token_f * scaled, axis=-1, keepdims=True)
    d_tokens = (rstd * scaled - token_f * rstd * rstd * rstd * mixed).astype(jnp.bfloat16)
    return (d_tokens, *grads)


def solution(mesh):
    placed = (
        P("sq", None),
        P(),
        P("sq", None),
        P("sq", None),
        P("sq", None),
        P("sq", None, None),
        P("sq", None, None),
        P("sq", None, None),
    )
    return jax.shard_map(
        local,
        mesh=mesh,
        in_specs=placed,
        out_specs=(P("sq", None), P("sq", None, None), P("sq", None, None), P("sq", None, None)),
        check_vma=False,
    )
```

```python
import jax
import jax.numpy as jnp
from jax import lax
from jax.experimental import pallas as pl
from jax.experimental.layout import Layout, with_layout_constraint
from jax.experimental.pallas import tpu as pltpu
from jax.sharding import PartitionSpec as P

QUARTERS = 4
CORE, PAIR, SIDE = 1, 2, 4
TILE = 8
PRODUCT_COLUMNS = 768

norm_eps = 1e-05
glu_alpha = 1.702


def contract_rows(left, right):
    return lax.dot_general(
        left, right, (((0,), (0,)), ((), ())), preferred_element_type=jnp.float32
    )


def contract_cols(left, right):
    return lax.dot_general(
        left, right, (((1,), (1,)), ((), ())), preferred_element_type=jnp.float32
    )


def row_major(value):
    return with_layout_constraint(value, Layout(major_to_minor=(0, 1)))


def behind(values, first):
    return lax.optimization_barrier((values, first))[0]


def fast_copy_kernel(weight_ref, out_ref, done):
    copy = pltpu.make_async_copy(weight_ref, out_ref, done)
    copy.start()
    copy.wait()


def fast_copy(weight):
    return pl.pallas_call(
        fast_copy_kernel,
        in_specs=[pl.BlockSpec(memory_space=pl.ANY)],
        out_specs=pl.BlockSpec(memory_space=pltpu.VMEM),
        out_shape=jax.ShapeDtypeStruct(weight.shape, weight.dtype),
        scratch_shapes=[pltpu.SemaphoreType.DMA],
        cost_estimate=pl.CostEstimate(
            flops=0, bytes_accessed=4 * weight.size, transcendentals=0
        ),
        compiler_params=pltpu.CompilerParams(vmem_limit_bytes=8 * 1024 * 1024),
    )(weight)


def product_kernel(left_ref, right_ref, out_ref, turned_ref, result_ref, sent):
    turned_ref[...] = left_ref[...].T
    width = right_ref.shape[1]
    copies = []
    for number, first in enumerate(range(0, width, PRODUCT_COLUMNS)):
        columns = slice(first, min(first + PRODUCT_COLUMNS, width))
        result_ref[:, columns] = jnp.dot(
            turned_ref[...], right_ref[:, columns], preferred_element_type=jnp.float32
        ).astype(result_ref.dtype)
        copies.append(
            pltpu.make_async_copy(
                result_ref.at[:, columns], out_ref.at[:, columns], sent.at[number]
            )
        )
        copies[-1].start()
    for copy in copies:
        copy.wait()


def weight_product(left, right):
    rows, hidden = left.shape
    width = right.shape[1]
    return pl.pallas_call(
        product_kernel,
        in_specs=[pl.BlockSpec(memory_space=pltpu.VMEM)] * 2,
        out_specs=pl.BlockSpec(memory_space=pl.ANY),
        out_shape=jax.ShapeDtypeStruct((hidden, width), jnp.bfloat16),
        scratch_shapes=[
            pltpu.VMEM((hidden, rows), jnp.bfloat16),
            pltpu.VMEM((hidden, width), jnp.bfloat16),
            pltpu.SemaphoreType.DMA((-(-width // PRODUCT_COLUMNS),)),
        ],
        cost_estimate=pl.CostEstimate(
            flops=2 * rows * hidden * width,
            bytes_accessed=2 * (rows * hidden + rows * width + hidden * width),
            transcendentals=0,
        ),
        compiler_params=pltpu.CompilerParams(vmem_limit_bytes=24 * 1024 * 1024),
    )(left, right)


def payload_kernel(tokens_ref, gain_ref, ids_ref, weight_ref, out_ref, rstd_ref):
    tok_count, width = tokens_ref.shape
    top_count = ids_ref.shape[0]
    expert_count = (out_ref.shape[1] - width) // 3
    token_f = tokens_ref[...].astype(jnp.float32)
    rstd = lax.rsqrt(jnp.mean(token_f * token_f, axis=-1, keepdims=True) + norm_eps)
    rstd_ref[...] = rstd
    out_ref[:, :width] = (token_f * rstd * gain_ref[...]).astype(jnp.bfloat16)
    experts = lax.broadcasted_iota(jnp.int32, (expert_count, tok_count), 0)
    weight = jnp.zeros((expert_count, tok_count), jnp.float32)
    for k in range(top_count):
        weight += jnp.where(ids_ref[k : k + 1, :] == experts, weight_ref[k : k + 1, :], 0.0)
    parts = []
    for _ in range(3):
        parts.append(weight.astype(jnp.bfloat16))
        weight = weight - parts[-1].astype(jnp.float32)
    parts = jnp.concatenate([part.astype(jnp.float32) for part in parts], axis=0)
    row = lax.broadcasted_iota(jnp.int32, (3 * expert_count, 3 * expert_count), 0)
    col = lax.broadcasted_iota(jnp.int32, (3 * expert_count, 3 * expert_count), 1)
    unit = (row == col).astype(jnp.bfloat16)
    turned = lax.dot_general(
        parts.astype(jnp.bfloat16),
        unit,
        (((0,), (0,)), ((), ())),
        preferred_element_type=jnp.float32,
    )
    out_ref[:, width:] = turned.astype(jnp.bfloat16)


def make_payload(tokens, norm_gain, expert_ids, combine_weight, expert_count):
    tok_count, width = tokens.shape
    return pl.pallas_call(
        payload_kernel,
        in_specs=[pl.BlockSpec(memory_space=pltpu.VMEM)] * 4,
        out_specs=[pl.BlockSpec(memory_space=pltpu.VMEM)] * 2,
        out_shape=[
            jax.ShapeDtypeStruct((tok_count, width + 3 * expert_count), jnp.bfloat16),
            jax.ShapeDtypeStruct((tok_count, 1), jnp.float32),
        ],
        cost_estimate=pl.CostEstimate(
            flops=4 * tok_count * width, bytes_accessed=4 * tok_count * width, transcendentals=0
        ),
    )(tokens, norm_gain[None, :], expert_ids.T, combine_weight.T)


def local(tokens, norm_gain, expert_ids, combine_weight, cotangent, w_gate, w_up, w_down):
    devices = lax.axis_size("sq")
    tok_count, top_count = expert_ids.shape
    width = tokens.shape[1]
    expert_count = devices // QUARTERS
    planes = expert_count // 2
    slot_count = tok_count * top_count * QUARTERS // devices + 1
    slots = -(-slot_count * planes // TILE) * TILE
    column = planes * tok_count
    kept = 2 * slots
    expert = lax.axis_index("sq") // QUARTERS
    plane = expert // 2

    def flip(value, bit):
        return lax.ppermute(row_major(value), "sq", [(i, i ^ bit) for i in range(devices)])

    def shift(value, by):
        step = by * 2 * QUARTERS
        pairs = [(i, (i + step) % devices) for i in range(devices)]
        return lax.ppermute(row_major(value), "sq", pairs)

    payload, rstd = make_payload(tokens, norm_gain, expert_ids, combine_weight, expert_count)

    lines = [
        [plane * 2 * QUARTERS + place for plane in range(planes)] for place in range(2 * QUARTERS)
    ]

    def gather_column(block):
        return row_major(
            lax.all_gather(block, "sq", axis=0, tiled=True, axis_index_groups=lines)
        )

    column_x = gather_column(payload)

    parts = column_x[:, width:].astype(jnp.float32).reshape(column, 3, expert_count)
    column_weight = parts[:, 0] + parts[:, 1] + parts[:, 2]
    slot_iota = lax.broadcasted_iota(jnp.int32, (slots, column), 0)
    earlier = lax.broadcasted_iota(jnp.int32, (column, column), 0) < lax.broadcasted_iota(
        jnp.int32, (column, column), 1
    )

    def choose(which):
        experts = jnp.arange(expert_count, dtype=jnp.int32)
        mine = jnp.sum(jnp.where(experts[None, :] == which, column_weight, 0.0), axis=1)
        mask = mine > 0.0
        slot = jnp.sum(jnp.where(earlier & mask[:, None], 1, 0), axis=0)
        hit = (slot_iota == slot[None, :]) & mask[None, :]
        row_weight = jnp.sum(jnp.where(hit, mine[None, :], 0.0), axis=1, keepdims=True)
        return hit.astype(jnp.bfloat16), row_weight

    own_select, own_weight = choose(expert)
    far_select, far_weight = choose(expert ^ 1)

    def rows_x(select):
        return jnp.dot(select, column_x[:, :width], preferred_element_type=jnp.float32).astype(
            jnp.bfloat16
        )

    own_x = rows_x(own_select)
    far_x = rows_x(far_select)
    side_x = flip(far_x, SIDE)
    pair_x = flip(own_x, PAIR)
    across_x = flip(far_x, PAIR | SIDE)
    column_cot = behind(gather_column(cotangent), (side_x, pair_x, across_x))

    def rows_dy(select, row_weight):
        rows = jnp.dot(select, column_cot, preferred_element_type=jnp.float32)
        return (rows * row_weight).astype(jnp.bfloat16)

    own_dy = rows_dy(own_select, own_weight)
    far_dy = rows_dy(far_select, far_weight)
    side_dy = flip(far_dy, SIDE)
    pair_dy = flip(own_dy, PAIR)

    def both_cores(first, second):
        rows = jnp.concatenate([first, second], axis=0)
        return jnp.concatenate([rows, flip(rows, CORE)], axis=0)

    gate_w = fast_copy(behind(w_gate[0], (own_dy, far_dy)).T).T
    up_w = w_up[0]

    def forward(x_in):
        gate = jnp.dot(x_in, gate_w, preferred_element_type=jnp.float32)
        up = jnp.dot(x_in, up_w, preferred_element_type=jnp.float32)
        return gate, up

    def hidden(gate, up, dy_e):
        sig = jax.nn.sigmoid(glu_alpha * gate)
        glu = gate * sig
        hid = (glu * (up + 1.0)).astype(jnp.bfloat16)
        d_hid = contract_cols(dy_e, down_w)
        d_up = (d_hid * glu).astype(jnp.bfloat16)
        d_gate = (d_hid * (up + 1.0) * (sig + glu_alpha * gate * sig * (1.0 - sig))).astype(
            jnp.bfloat16
        )
        return hid, d_gate, d_up

    def row_gradient(d_gate, d_up, first, last):
        return (
            contract_cols(d_gate, gate_w[first:last]) + contract_cols(d_up, up_w[first:last])
        ).astype(jnp.bfloat16)

    own_x, side_x, pair_x, across_x = behind((own_x, side_x, pair_x, across_x), (own_dy, far_dy))
    chip_x = both_cores(own_x, side_x)
    pair_x = both_cores(pair_x, across_x)
    chip_forward = forward(chip_x)
    down_w = fast_copy(behind(w_down[0], chip_forward))
    side_dy, pair_dy = behind((side_dy, pair_dy), chip_forward)
    across_dy = flip(side_dy, PAIR)
    chip_dy = both_cores(own_dy, side_dy)
    pair_forward = forward(behind(pair_x, chip_dy))
    chip_hid, chip_d_gate, chip_d_up = hidden(*chip_forward, chip_dy)
    chip_rows = row_gradient(chip_d_gate, chip_d_up, 0, width)
    chip_sum = chip_rows[:kept].astype(jnp.float32) + flip(chip_rows[kept:], CORE).astype(
        jnp.float32
    )
    side_sum = flip(chip_sum[slots:].astype(jnp.bfloat16), SIDE)

    pair_core_dy = flip(pair_dy, CORE)
    across_dy = behind(across_dy, (chip_rows, pair_forward))
    pair_dy = jnp.concatenate([pair_dy, across_dy, pair_core_dy, flip(across_dy, CORE)], axis=0)
    pair_hid, pair_d_gate, pair_d_up = hidden(*pair_forward, pair_dy)

    cut = width // 2 // 256 * 256
    spans = [(0, cut), (cut, width)]

    def core_sum(rows, from_core):
        total = rows[:kept].astype(jnp.float32) + from_core.astype(jnp.float32)
        return total.astype(jnp.bfloat16)

    def to_pair(rows):
        return flip(rows[:slots], PAIR), flip(rows[slots:], PAIR | SIDE)

    rows_first = row_gradient(*behind((pair_d_gate, pair_d_up), chip_sum), *spans[0])
    core_first = flip(rows_first[kept:], CORE)
    rows_second = row_gradient(*behind((pair_d_gate, pair_d_up), rows_first), *spans[1])
    core_second = flip(rows_second[kept:], CORE)
    sum_first = core_sum(rows_first, core_first)
    sent_first = to_pair(sum_first)

    x_in = jnp.concatenate([chip_x, pair_x], axis=0)
    dy_e = jnp.concatenate([chip_dy, pair_dy], axis=0)
    hid = jnp.concatenate([chip_hid, pair_hid], axis=0)
    d_gate = jnp.concatenate([chip_d_gate, pair_d_gate], axis=0)
    d_up = jnp.concatenate([chip_d_up, pair_d_up], axis=0)

    def to_column(span, from_pair, from_across):
        first, last = span
        own_rows = chip_sum[:slots, first:last] + from_pair.astype(jnp.float32)
        far_rows = side_sum[:, first:last].astype(jnp.float32) + from_across.astype(jnp.float32)
        return row_major(
            contract_rows(own_select, own_rows.astype(jnp.bfloat16))
            + contract_rows(far_select, far_rows.astype(jnp.bfloat16))
        )

    def to_tokens(d_column):
        blocks = d_column.reshape(planes, tok_count, d_column.shape[1])
        total = lax.dynamic_index_in_dim(blocks, plane, 0, False)
        got = []
        for s in range(1, planes):
            block = lax.dynamic_index_in_dim(blocks, (plane + s) % planes, 0, False)
            got.append(shift(block.astype(jnp.bfloat16), s))
        return total, got

    def added(total, got):
        for block in got:
            total = total + block.astype(jnp.float32)
        return total

    def weight_gradient(hidden_rows, model_rows, first):
        return weight_product(*behind((hidden_rows, model_rows), first))

    grad_gate = weight_gradient(d_gate, x_in, (sum_first, rows_second, chip_sum))
    sum_second = core_sum(*behind((rows_second, core_second), grad_gate))
    sent_second = to_pair(sum_second)
    d_column = to_column(spans[0], *behind(sent_first, grad_gate))
    first_half = to_tokens(d_column)
    grad_up = weight_gradient(d_up, x_in, d_column)
    first_half = added(*behind(first_half, grad_up))
    second_half = to_tokens(to_column(spans[1], *behind(sent_second, first_half)))
    grad_down = weight_gradient(hid, dy_e, first_half)
    second_half = added(*behind(second_half, grad_down))
    grads = [grad_gate.T[None], grad_up.T[None], grad_down[None]]
    d_normed = jnp.concatenate([first_half, second_half], axis=1)

    token_f = row_major(tokens).astype(jnp.float32)
    scaled = d_normed * norm_gain
    mixed = jnp.mean(token_f * scaled, axis=-1, keepdims=True)
    d_tokens = (rstd * scaled - token_f * rstd * rstd * rstd * mixed).astype(jnp.bfloat16)
    return (d_tokens, *grads)


def solution(mesh):
    placed = (
        P("sq", None),
        P(),
        P("sq", None),
        P("sq", None),
        P("sq", None),
        P("sq", None, None),
        P("sq", None, None),
        P("sq", None, None),
    )
    return jax.shard_map(
        local,
        mesh=mesh,
        in_specs=placed,
        out_specs=(P("sq", None), P("sq", None, None), P("sq", None, None), P("sq", None, None)),
        check_vma=False,
    )
```

```python
import jax
import jax.numpy as jnp
from jax import lax
from jax.experimental import pallas as pl
from jax.experimental.layout import Layout, with_layout_constraint
from jax.experimental.pallas import tpu as pltpu
from jax.sharding import PartitionSpec as P

QUARTERS = 4
CORE, PAIR, SIDE = 1, 2, 4
TILE = 8
PRODUCT_COLUMNS = 768

norm_eps = 1e-05
glu_alpha = 1.702


def contract_rows(left, right):
    return lax.dot_general(
        left, right, (((0,), (0,)), ((), ())), preferred_element_type=jnp.float32
    )


def contract_cols(left, right):
    return lax.dot_general(
        left, right, (((1,), (1,)), ((), ())), preferred_element_type=jnp.float32
    )


def row_major(value):
    return with_layout_constraint(value, Layout(major_to_minor=(0, 1)))


def behind(values, first):
    return lax.optimization_barrier((values, first))[0]


def fast_copy_kernel(weight_ref, out_ref, done):
    copy = pltpu.make_async_copy(weight_ref, out_ref, done)
    copy.start()
    copy.wait()


def fast_copy(weight):
    return pl.pallas_call(
        fast_copy_kernel,
        in_specs=[pl.BlockSpec(memory_space=pl.ANY)],
        out_specs=pl.BlockSpec(memory_space=pltpu.VMEM),
        out_shape=jax.ShapeDtypeStruct(weight.shape, weight.dtype),
        scratch_shapes=[pltpu.SemaphoreType.DMA],
        cost_estimate=pl.CostEstimate(
            flops=0, bytes_accessed=4 * weight.size, transcendentals=0
        ),
        compiler_params=pltpu.CompilerParams(vmem_limit_bytes=8 * 1024 * 1024),
    )(weight)


def product_kernel(left_ref, right_ref, out_ref, turned_ref, result_ref, sent):
    turned_ref[...] = left_ref[...].T
    width = right_ref.shape[1]
    copies = []
    for number, first in enumerate(range(0, width, PRODUCT_COLUMNS)):
        columns = slice(first, min(first + PRODUCT_COLUMNS, width))
        result_ref[:, columns] = jnp.dot(
            turned_ref[...], right_ref[:, columns], preferred_element_type=jnp.float32
        ).astype(result_ref.dtype)
        copies.append(
            pltpu.make_async_copy(
                result_ref.at[:, columns], out_ref.at[:, columns], sent.at[number]
            )
        )
        copies[-1].start()
    for copy in copies:
        copy.wait()


def weight_product(left, right):
    rows, hidden = left.shape
    width = right.shape[1]
    return pl.pallas_call(
        product_kernel,
        in_specs=[pl.BlockSpec(memory_space=pltpu.VMEM)] * 2,
        out_specs=pl.BlockSpec(memory_space=pl.ANY),
        out_shape=jax.ShapeDtypeStruct((hidden, width), jnp.bfloat16),
        scratch_shapes=[
            pltpu.VMEM((hidden, rows), jnp.bfloat16),
            pltpu.VMEM((hidden, width), jnp.bfloat16),
            pltpu.SemaphoreType.DMA((-(-width // PRODUCT_COLUMNS),)),
        ],
        cost_estimate=pl.CostEstimate(
            flops=2 * rows * hidden * width,
            bytes_accessed=2 * (rows * hidden + rows * width + hidden * width),
            transcendentals=0,
        ),
        compiler_params=pltpu.CompilerParams(vmem_limit_bytes=24 * 1024 * 1024),
    )(left, right)


def three_parts(value):
    first = lax.reduce_precision(value, 8, 7)
    rest = value - first
    second = lax.reduce_precision(rest, 8, 7)
    return [part.astype(jnp.bfloat16) for part in (first, second, rest - second)]


def local(tokens, norm_gain, expert_ids, combine_weight, cotangent, w_gate, w_up, w_down):
    devices = lax.axis_size("sq")
    tok_count, top_count = expert_ids.shape
    width = tokens.shape[1]
    expert_count = devices // QUARTERS
    planes = expert_count // 2
    slot_count = tok_count * top_count * QUARTERS // devices + 1
    slots = -(-slot_count * planes // TILE) * TILE
    column = planes * tok_count
    kept = 2 * slots
    expert = lax.axis_index("sq") // QUARTERS
    plane = expert // 2

    def flip(value, bit):
        return lax.ppermute(row_major(value), "sq", [(i, i ^ bit) for i in range(devices)])

    def shift(value, by):
        step = by * 2 * QUARTERS
        pairs = [(i, (i + step) % devices) for i in range(devices)]
        return lax.ppermute(row_major(value), "sq", pairs)

    token_f = row_major(tokens).astype(jnp.float32)
    rstd = lax.rsqrt(jnp.mean(token_f * token_f, axis=-1, keepdims=True) + norm_eps)
    normed = (token_f * rstd * norm_gain).astype(jnp.bfloat16)

    picked = expert_ids[:, :, None] == jnp.arange(expert_count, dtype=jnp.int32)[None, None, :]
    weight = jnp.sum(jnp.where(picked, combine_weight[:, :, None], 0.0), axis=1)
    payload = row_major(jnp.concatenate([normed] + three_parts(weight), axis=1))

    lines = [
        [plane * 2 * QUARTERS + place for plane in range(planes)] for place in range(2 * QUARTERS)
    ]

    def gather_column(block):
        return row_major(
            lax.all_gather(block, "sq", axis=0, tiled=True, axis_index_groups=lines)
        )

    column_x = gather_column(payload)

    parts = column_x[:, width:].astype(jnp.float32).reshape(column, 3, expert_count)
    column_weight = parts[:, 0] + parts[:, 1] + parts[:, 2]
    slot_iota = lax.broadcasted_iota(jnp.int32, (slots, column), 0)
    earlier = lax.broadcasted_iota(jnp.int32, (column, column), 0) < lax.broadcasted_iota(
        jnp.int32, (column, column), 1
    )

    def choose(which):
        experts = jnp.arange(expert_count, dtype=jnp.int32)
        mine = jnp.sum(jnp.where(experts[None, :] == which, column_weight, 0.0), axis=1)
        mask = mine > 0.0
        slot = jnp.sum(jnp.where(earlier & mask[:, None], 1, 0), axis=0)
        hit = (slot_iota == slot[None, :]) & mask[None, :]
        row_weight = jnp.sum(jnp.where(hit, mine[None, :], 0.0), axis=1, keepdims=True)
        return hit.astype(jnp.bfloat16), row_weight

    own_select, own_weight = choose(expert)
    far_select, far_weight = choose(expert ^ 1)

    def rows_x(select):
        return jnp.dot(select, column_x[:, :width], preferred_element_type=jnp.float32).astype(
            jnp.bfloat16
        )

    own_x = rows_x(own_select)
    far_x = rows_x(far_select)
    side_x = flip(far_x, SIDE)
    pair_x = flip(own_x, PAIR)
    across_x = flip(far_x, PAIR | SIDE)
    column_cot = behind(gather_column(cotangent), (side_x, pair_x, across_x))

    def rows_dy(select, row_weight):
        rows = jnp.dot(select, column_cot, preferred_element_type=jnp.float32)
        return (rows * row_weight).astype(jnp.bfloat16)

    own_dy = rows_dy(own_select, own_weight)
    far_dy = rows_dy(far_select, far_weight)
    side_dy = flip(far_dy, SIDE)
    pair_dy = flip(own_dy, PAIR)
    across_dy = flip(far_dy, PAIR | SIDE)

    def both_cores(first, second):
        rows = jnp.concatenate([first, second], axis=0)
        return jnp.concatenate([rows, flip(rows, CORE)], axis=0)

    gate_w = fast_copy(behind(w_gate[0], (own_dy, far_dy)).T).T
    up_w = w_up[0]

    def forward(x_in):
        gate = jnp.dot(x_in, gate_w, preferred_element_type=jnp.float32)
        up = jnp.dot(x_in, up_w, preferred_element_type=jnp.float32)
        return gate, up

    def hidden(gate, up, dy_e):
        sig = jax.nn.sigmoid(glu_alpha * gate)
        glu = gate * sig
        hid = (glu * (up + 1.0)).astype(jnp.bfloat16)
        d_hid = contract_cols(dy_e, down_w)
        d_up = (d_hid * glu).astype(jnp.bfloat16)
        d_gate = (d_hid * (up + 1.0) * (sig + glu_alpha * gate * sig * (1.0 - sig))).astype(
            jnp.bfloat16
        )
        return hid, d_gate, d_up

    def row_gradient(d_gate, d_up, first, last):
        return (
            contract_cols(d_gate, gate_w[first:last]) + contract_cols(d_up, up_w[first:last])
        ).astype(jnp.bfloat16)

    chip_x = behind(both_cores(own_x, side_x), (own_dy, far_dy))
    pair_x = both_cores(pair_x, across_x)
    chip_forward = forward(chip_x)
    down_w = fast_copy(behind(w_down[0], chip_forward))
    pair_forward = forward(behind(pair_x, chip_forward))
    side_dy, pair_dy, across_dy = behind(
        (side_dy, pair_dy, across_dy), (chip_forward, pair_forward)
    )
    chip_dy = both_cores(own_dy, side_dy)
    pair_dy = both_cores(pair_dy, across_dy)
    chip_hid, chip_d_gate, chip_d_up = hidden(*chip_forward, chip_dy)
    chip_rows = row_gradient(chip_d_gate, chip_d_up, 0, width)
    chip_sum = chip_rows[:kept].astype(jnp.float32) + flip(chip_rows[kept:], CORE).astype(
        jnp.float32
    )
    side_sum = flip(chip_sum[slots:].astype(jnp.bfloat16), SIDE)

    pair_hid, pair_d_gate, pair_d_up = hidden(*pair_forward, behind(pair_dy, chip_rows))

    cut = -(-width // 2 // 256) * 256
    spans = [(0, cut), (cut, width)]

    def core_sum(rows, from_core):
        total = rows[:kept].astype(jnp.float32) + from_core.astype(jnp.float32)
        return total.astype(jnp.bfloat16)

    def to_pair(rows):
        return flip(rows[:slots], PAIR), flip(rows[slots:], PAIR | SIDE)

    rows_first = row_gradient(*behind((pair_d_gate, pair_d_up), chip_sum), *spans[0])
    core_first = flip(rows_first[kept:], CORE)
    rows_second = row_gradient(*behind((pair_d_gate, pair_d_up), rows_first), *spans[1])
    core_second = flip(rows_second[kept:], CORE)
    sum_first = core_sum(rows_first, core_first)
    sent_first = to_pair(sum_first)

    x_in = jnp.concatenate([chip_x, pair_x], axis=0)
    dy_e = jnp.concatenate([chip_dy, pair_dy], axis=0)
    hid = jnp.concatenate([chip_hid, pair_hid], axis=0)
    d_gate = jnp.concatenate([chip_d_gate, pair_d_gate], axis=0)
    d_up = jnp.concatenate([chip_d_up, pair_d_up], axis=0)

    def to_column(span, from_pair, from_across):
        first, last = span
        own_rows = chip_sum[:slots, first:last] + from_pair.astype(jnp.float32)
        far_rows = side_sum[:, first:last].astype(jnp.float32) + from_across.astype(jnp.float32)
        return row_major(
            contract_rows(own_select, own_rows.astype(jnp.bfloat16))
            + contract_rows(far_select, far_rows.astype(jnp.bfloat16))
        )

    def to_tokens(d_column):
        blocks = d_column.reshape(planes, tok_count, d_column.shape[1])
        total = lax.dynamic_index_in_dim(blocks, plane, 0, False)
        got = []
        for s in range(1, planes):
            block = lax.dynamic_index_in_dim(blocks, (plane + s) % planes, 0, False)
            got.append(shift(block.astype(jnp.bfloat16), s))
        return total, got

    def added(total, got):
        for block in got:
            total = total + block.astype(jnp.float32)
        return total

    def weight_gradient(hidden_rows, model_rows, first):
        return weight_product(*behind((hidden_rows, model_rows), first))

    grad_gate = weight_gradient(d_gate, x_in, (sum_first, rows_second, chip_sum))
    sum_second = core_sum(*behind((rows_second, core_second), grad_gate))
    sent_second = to_pair(sum_second)
    d_column = to_column(spans[0], *behind(sent_first, grad_gate))
    first_half = to_tokens(d_column)
    grad_up = weight_gradient(d_up, x_in, d_column)
    first_half = added(*behind(first_half, grad_up))
    d_column = to_column(spans[1], *behind(sent_second, first_half))
    second_half = to_tokens(d_column)
    grad_down = weight_gradient(hid, dy_e, d_column)
    second_half = added(*behind(second_half, grad_down))
    grads = [grad_gate.T[None], grad_up.T[None], grad_down[None]]
    d_normed = jnp.concatenate([first_half, second_half], axis=1)

    scaled = d_normed * norm_gain
    mixed = jnp.mean(token_f * scaled, axis=-1, keepdims=True)
    d_tokens = (rstd * scaled - token_f * rstd * rstd * rstd * mixed).astype(jnp.bfloat16)
    return (d_tokens, *grads)


def solution(mesh):
    placed = (
        P("sq", None),
        P(),
        P("sq", None),
        P("sq", None),
        P("sq", None),
        P("sq", None, None),
        P("sq", None, None),
        P("sq", None, None),
    )
    return jax.shard_map(
        local,
        mesh=mesh,
        in_specs=placed,
        out_specs=(P("sq", None), P("sq", None, None), P("sq", None, None), P("sq", None, None)),
        check_vma=False,
    )
```

```python
import jax
import jax.numpy as jnp
from jax import lax
from jax.experimental import pallas as pl
from jax.experimental.layout import Layout, with_layout_constraint
from jax.experimental.pallas import tpu as pltpu
from jax.sharding import PartitionSpec as P

QUARTERS = 4
CORE, PAIR, SIDE = 1, 2, 4
TILE = 8
PRODUCT_COLUMNS = 768

norm_eps = 1e-05
glu_alpha = 1.702


def contract_rows(left, right):
    return lax.dot_general(
        left, right, (((0,), (0,)), ((), ())), preferred_element_type=jnp.float32
    )


def contract_cols(left, right):
    return lax.dot_general(
        left, right, (((1,), (1,)), ((), ())), preferred_element_type=jnp.float32
    )


def row_major(value):
    return with_layout_constraint(value, Layout(major_to_minor=(0, 1)))


def behind(values, first):
    return lax.optimization_barrier((values, first))[0]


def fast_copy_kernel(weight_ref, out_ref, done):
    copy = pltpu.make_async_copy(weight_ref, out_ref, done)
    copy.start()
    copy.wait()


def fast_copy(weight):
    return pl.pallas_call(
        fast_copy_kernel,
        in_specs=[pl.BlockSpec(memory_space=pl.ANY)],
        out_specs=pl.BlockSpec(memory_space=pltpu.VMEM),
        out_shape=jax.ShapeDtypeStruct(weight.shape, weight.dtype),
        scratch_shapes=[pltpu.SemaphoreType.DMA],
        cost_estimate=pl.CostEstimate(
            flops=0, bytes_accessed=4 * weight.size, transcendentals=0
        ),
        compiler_params=pltpu.CompilerParams(vmem_limit_bytes=8 * 1024 * 1024),
    )(weight)


def product_kernel(left_ref, right_ref, out_ref, turned_ref, result_ref, sent):
    turned_ref[...] = left_ref[...].T
    width = right_ref.shape[1]
    copies = []
    for number, first in enumerate(range(0, width, PRODUCT_COLUMNS)):
        columns = slice(first, min(first + PRODUCT_COLUMNS, width))
        result_ref[:, columns] = jnp.dot(
            turned_ref[...], right_ref[:, columns], preferred_element_type=jnp.float32
        ).astype(result_ref.dtype)
        copies.append(
            pltpu.make_async_copy(
                result_ref.at[:, columns], out_ref.at[:, columns], sent.at[number]
            )
        )
        copies[-1].start()
    for copy in copies:
        copy.wait()


def weight_product(left, right):
    rows, hidden = left.shape
    width = right.shape[1]
    return pl.pallas_call(
        product_kernel,
        in_specs=[pl.BlockSpec(memory_space=pltpu.VMEM)] * 2,
        out_specs=pl.BlockSpec(memory_space=pl.ANY),
        out_shape=jax.ShapeDtypeStruct((hidden, width), jnp.bfloat16),
        scratch_shapes=[
            pltpu.VMEM((hidden, rows), jnp.bfloat16),
            pltpu.VMEM((hidden, width), jnp.bfloat16),
            pltpu.SemaphoreType.DMA((-(-width // PRODUCT_COLUMNS),)),
        ],
        cost_estimate=pl.CostEstimate(
            flops=2 * rows * hidden * width,
            bytes_accessed=2 * (rows * hidden + rows * width + hidden * width),
            transcendentals=0,
        ),
        compiler_params=pltpu.CompilerParams(vmem_limit_bytes=24 * 1024 * 1024),
    )(left, right)


def three_parts(value):
    first = lax.reduce_precision(value, 8, 7)
    rest = value - first
    second = lax.reduce_precision(rest, 8, 7)
    return [part.astype(jnp.bfloat16) for part in (first, second, rest - second)]


def local(tokens, norm_gain, expert_ids, combine_weight, cotangent, w_gate, w_up, w_down):
    devices = lax.axis_size("sq")
    tok_count, top_count = expert_ids.shape
    width = tokens.shape[1]
    expert_count = devices // QUARTERS
    planes = expert_count // 2
    slot_count = tok_count * top_count * QUARTERS // devices + 1
    slots = -(-slot_count * planes // TILE) * TILE
    column = planes * tok_count
    kept = 2 * slots
    expert = lax.axis_index("sq") // QUARTERS
    plane = expert // 2

    def flip(value, bit):
        return lax.ppermute(row_major(value), "sq", [(i, i ^ bit) for i in range(devices)])

    def shift(value, by):
        step = by * 2 * QUARTERS
        pairs = [(i, (i + step) % devices) for i in range(devices)]
        return lax.ppermute(row_major(value), "sq", pairs)

    token_f = row_major(tokens).astype(jnp.float32)
    rstd = lax.rsqrt(jnp.mean(token_f * token_f, axis=-1, keepdims=True) + norm_eps)
    normed = (token_f * rstd * norm_gain).astype(jnp.bfloat16)

    picked = expert_ids[:, :, None] == jnp.arange(expert_count, dtype=jnp.int32)[None, None, :]
    weight = jnp.sum(jnp.where(picked, combine_weight[:, :, None], 0.0), axis=1)
    payload = row_major(jnp.concatenate([normed] + three_parts(weight), axis=1))

    lines = [
        [plane * 2 * QUARTERS + place for plane in range(planes)] for place in range(2 * QUARTERS)
    ]

    def gather_column(block):
        return row_major(
            lax.all_gather(block, "sq", axis=0, tiled=True, axis_index_groups=lines)
        )

    column_x = gather_column(payload)

    parts = column_x[:, width:].astype(jnp.float32).reshape(column, 3, expert_count)
    column_weight = parts[:, 0] + parts[:, 1] + parts[:, 2]
    slot_iota = lax.broadcasted_iota(jnp.int32, (slots, column), 0)
    earlier = lax.broadcasted_iota(jnp.int32, (column, column), 0) < lax.broadcasted_iota(
        jnp.int32, (column, column), 1
    )

    def choose(which):
        experts = jnp.arange(expert_count, dtype=jnp.int32)
        mine = jnp.sum(jnp.where(experts[None, :] == which, column_weight, 0.0), axis=1)
        mask = mine > 0.0
        slot = jnp.sum(jnp.where(earlier & mask[:, None], 1, 0), axis=0)
        hit = (slot_iota == slot[None, :]) & mask[None, :]
        row_weight = jnp.sum(jnp.where(hit, mine[None, :], 0.0), axis=1, keepdims=True)
        return hit.astype(jnp.bfloat16), row_weight

    own_select, own_weight = choose(expert)
    far_select, far_weight = choose(expert ^ 1)

    def rows_x(select):
        return jnp.dot(select, column_x[:, :width], preferred_element_type=jnp.float32).astype(
            jnp.bfloat16
        )

    own_x = rows_x(own_select)
    far_x = rows_x(far_select)
    side_x = flip(far_x, SIDE)
    pair_x = flip(own_x, PAIR)
    across_x = flip(far_x, PAIR | SIDE)
    column_cot = behind(gather_column(cotangent), (side_x, pair_x, across_x))

    def rows_dy(select, row_weight):
        rows = jnp.dot(select, column_cot, preferred_element_type=jnp.float32)
        return (rows * row_weight).astype(jnp.bfloat16)

    own_dy = rows_dy(own_select, own_weight)
    far_dy = rows_dy(far_select, far_weight)
    side_dy = flip(far_dy, SIDE)
    pair_dy = flip(own_dy, PAIR)

    def both_cores(first, second):
        rows = jnp.concatenate([first, second], axis=0)
        return jnp.concatenate([rows, flip(rows, CORE)], axis=0)

    gate_w = fast_copy(behind(w_gate[0], (own_dy, far_dy)).T).T
    up_w = w_up[0]
    down_w = fast_copy(behind(w_down[0], gate_w))

    def forward(x_in):
        gate = jnp.dot(x_in, gate_w, preferred_element_type=jnp.float32)
        up = jnp.dot(x_in, up_w, preferred_element_type=jnp.float32)
        return gate, up

    def hidden(gate, up, dy_e):
        sig = jax.nn.sigmoid(glu_alpha * gate)
        glu = gate * sig
        hid = (glu * (up + 1.0)).astype(jnp.bfloat16)
        d_hid = contract_cols(dy_e, down_w)
        d_up = (d_hid * glu).astype(jnp.bfloat16)
        d_gate = (d_hid * (up + 1.0) * (sig + glu_alpha * gate * sig * (1.0 - sig))).astype(
            jnp.bfloat16
        )
        return hid, d_gate, d_up

    def row_gradient(d_gate, d_up, first, last):
        return (
            contract_cols(d_gate, gate_w[first:last]) + contract_cols(d_up, up_w[first:last])
        ).astype(jnp.bfloat16)

    own_x, side_x, pair_x, across_x = behind((own_x, side_x, pair_x, across_x), (own_dy, far_dy))
    chip_x = both_cores(own_x, side_x)
    pair_x = both_cores(pair_x, across_x)
    chip_forward = forward(chip_x)
    side_dy, pair_dy = behind((side_dy, pair_dy), chip_forward)
    across_dy = flip(side_dy, PAIR)
    chip_dy = both_cores(own_dy, side_dy)
    pair_forward = forward(behind(pair_x, chip_dy))
    chip_hid, chip_d_gate, chip_d_up = hidden(*chip_forward, chip_dy)
    chip_rows = row_gradient(chip_d_gate, chip_d_up, 0, width)
    chip_sum = chip_rows[:kept].astype(jnp.float32) + flip(chip_rows[kept:], CORE).astype(
        jnp.float32
    )
    side_ready = chip_sum[slots:].astype(jnp.bfloat16)
    side_sum = flip(side_ready, SIDE)

    pair_core_dy = flip(pair_dy, CORE)
    across_dy = behind(across_dy, (chip_sum, pair_forward))
    pair_dy = jnp.concatenate([pair_dy, across_dy, pair_core_dy, flip(across_dy, CORE)], axis=0)
    pair_hid, pair_d_gate, pair_d_up = hidden(*pair_forward, pair_dy)

    cut = width // 2 // 128 * 128
    spans = [(0, cut), (cut, width)]

    def core_sum(rows, from_core):
        total = rows[:kept].astype(jnp.float32) + from_core.astype(jnp.float32)
        return total.astype(jnp.bfloat16)

    def to_pair(rows):
        return flip(rows[:slots], PAIR), flip(rows[slots:], PAIR | SIDE)

    rows_first = row_gradient(*behind((pair_d_gate, pair_d_up), side_ready), *spans[0])
    core_first = flip(rows_first[kept:], CORE)
    rows_second = row_gradient(*behind((pair_d_gate, pair_d_up), rows_first), *spans[1])
    sum_first = core_sum(rows_first, core_first)
    core_second = flip(behind(rows_second[kept:], sum_first), CORE)
    sent_first = to_pair(sum_first)

    x_in = jnp.concatenate([chip_x, pair_x], axis=0)
    dy_e = jnp.concatenate([chip_dy, pair_dy], axis=0)
    hid = jnp.concatenate([chip_hid, pair_hid], axis=0)
    d_gate = jnp.concatenate([chip_d_gate, pair_d_gate], axis=0)
    d_up = jnp.concatenate([chip_d_up, pair_d_up], axis=0)

    def to_column(span, from_pair, from_across):
        first, last = span
        own_rows = chip_sum[:slots, first:last] + from_pair.astype(jnp.float32)
        far_rows = side_sum[:, first:last].astype(jnp.float32) + from_across.astype(jnp.float32)
        return row_major(
            contract_rows(own_select, own_rows.astype(jnp.bfloat16))
            + contract_rows(far_select, far_rows.astype(jnp.bfloat16))
        )

    def to_tokens(d_column):
        blocks = d_column.reshape(planes, tok_count, d_column.shape[1])
        total = lax.dynamic_index_in_dim(blocks, plane, 0, False)
        got = []
        for s in range(1, planes):
            block = lax.dynamic_index_in_dim(blocks, (plane + s) % planes, 0, False)
            got.append(shift(block.astype(jnp.bfloat16), s))
        return total, got

    def added(total, got):
        for block in got:
            total = total + block.astype(jnp.float32)
        return total

    def weight_gradient(hidden_rows, model_rows, first):
        return weight_product(*behind((hidden_rows, model_rows), first))

    grad_gate = weight_gradient(d_gate, x_in, (sum_first, rows_second, chip_sum))
    sum_second = core_sum(*behind((rows_second, core_second), grad_gate))
    sent_second = to_pair(sum_second)
    d_column = to_column(spans[0], *behind(sent_first, (grad_gate, sum_second)))
    first_half = to_tokens(d_column)
    grad_up = weight_gradient(d_up, x_in, d_column)
    first_half = added(*behind(first_half, grad_up))
    d_column = to_column(spans[1], *behind(sent_second, first_half))
    second_half = to_tokens(d_column)
    grad_down = weight_gradient(hid, dy_e, d_column)
    second_half = added(*behind(second_half, grad_down))
    grads = [grad_gate.T[None], grad_up.T[None], grad_down[None]]
    d_normed = jnp.concatenate([first_half, second_half], axis=1)

    scaled = d_normed * norm_gain
    mixed = jnp.mean(token_f * scaled, axis=-1, keepdims=True)
    d_tokens = (rstd * scaled - token_f * rstd * rstd * rstd * mixed).astype(jnp.bfloat16)
    return (d_tokens, *grads)


def solution(mesh):
    placed = (
        P("sq", None),
        P(),
        P("sq", None),
        P("sq", None),
        P("sq", None),
        P("sq", None, None),
        P("sq", None, None),
        P("sq", None, None),
    )
    return jax.shard_map(
        local,
        mesh=mesh,
        in_specs=placed,
        out_specs=(P("sq", None), P("sq", None, None), P("sq", None, None), P("sq", None, None)),
        check_vma=False,
    )
```

```python
import jax
import jax.numpy as jnp
from jax import lax
from jax.experimental import pallas as pl
from jax.experimental.layout import Layout, with_layout_constraint
from jax.experimental.pallas import tpu as pltpu
from jax.sharding import PartitionSpec as P

QUARTERS = 4
CORE, PAIR, SIDE = 1, 2, 4
TILE = 8
PRODUCT_COLUMNS = 768

norm_eps = 1e-05
glu_alpha = 1.702


def contract_rows(left, right):
    return lax.dot_general(
        left, right, (((0,), (0,)), ((), ())), preferred_element_type=jnp.float32
    )


def contract_cols(left, right):
    return lax.dot_general(
        left, right, (((1,), (1,)), ((), ())), preferred_element_type=jnp.float32
    )


def row_major(value):
    return with_layout_constraint(value, Layout(major_to_minor=(0, 1)))


def behind(values, first):
    return lax.optimization_barrier((values, first))[0]


def fast_copy_kernel(weight_ref, out_ref, done):
    copy = pltpu.make_async_copy(weight_ref, out_ref, done)
    copy.start()
    copy.wait()


def fast_copy(weight):
    return pl.pallas_call(
        fast_copy_kernel,
        in_specs=[pl.BlockSpec(memory_space=pl.ANY)],
        out_specs=pl.BlockSpec(memory_space=pltpu.VMEM),
        out_shape=jax.ShapeDtypeStruct(weight.shape, weight.dtype),
        scratch_shapes=[pltpu.SemaphoreType.DMA],
        cost_estimate=pl.CostEstimate(
            flops=0, bytes_accessed=4 * weight.size, transcendentals=0
        ),
        compiler_params=pltpu.CompilerParams(vmem_limit_bytes=8 * 1024 * 1024),
    )(weight)


def product_kernel(left_ref, right_ref, out_ref, turned_ref, result_ref, sent):
    turned_ref[...] = left_ref[...].T
    width = right_ref.shape[1]
    copies = []
    for number, first in enumerate(range(0, width, PRODUCT_COLUMNS)):
        columns = slice(first, min(first + PRODUCT_COLUMNS, width))
        result_ref[:, columns] = jnp.dot(
            turned_ref[...], right_ref[:, columns], preferred_element_type=jnp.float32
        ).astype(result_ref.dtype)
        copies.append(
            pltpu.make_async_copy(
                result_ref.at[:, columns], out_ref.at[:, columns], sent.at[number]
            )
        )
        copies[-1].start()
    for copy in copies:
        copy.wait()


def weight_product(left, right):
    rows, hidden = left.shape
    width = right.shape[1]
    return pl.pallas_call(
        product_kernel,
        in_specs=[pl.BlockSpec(memory_space=pltpu.VMEM)] * 2,
        out_specs=pl.BlockSpec(memory_space=pl.ANY),
        out_shape=jax.ShapeDtypeStruct((hidden, width), jnp.bfloat16),
        scratch_shapes=[
            pltpu.VMEM((hidden, rows), jnp.bfloat16),
            pltpu.VMEM((hidden, width), jnp.bfloat16),
            pltpu.SemaphoreType.DMA((-(-width // PRODUCT_COLUMNS),)),
        ],
        cost_estimate=pl.CostEstimate(
            flops=2 * rows * hidden * width,
            bytes_accessed=2 * (rows * hidden + rows * width + hidden * width),
            transcendentals=0,
        ),
        compiler_params=pltpu.CompilerParams(vmem_limit_bytes=24 * 1024 * 1024),
    )(left, right)


def three_parts(value):
    first = lax.reduce_precision(value, 8, 7)
    rest = value - first
    second = lax.reduce_precision(rest, 8, 7)
    return [part.astype(jnp.bfloat16) for part in (first, second, rest - second)]


def local(tokens, norm_gain, expert_ids, combine_weight, cotangent, w_gate, w_up, w_down):
    devices = lax.axis_size("sq")
    tok_count, top_count = expert_ids.shape
    width = tokens.shape[1]
    expert_count = devices // QUARTERS
    planes = expert_count // 2
    slot_count = tok_count * top_count * QUARTERS // devices + 1
    slots = -(-slot_count * planes // TILE) * TILE
    column = planes * tok_count
    kept = 2 * slots
    expert = lax.axis_index("sq") // QUARTERS
    plane = expert // 2

    def flip(value, bit):
        return lax.ppermute(row_major(value), "sq", [(i, i ^ bit) for i in range(devices)])

    def shift(value, by):
        step = by * 2 * QUARTERS
        pairs = [(i, (i + step) % devices) for i in range(devices)]
        return lax.ppermute(row_major(value), "sq", pairs)

    token_f = row_major(tokens).astype(jnp.float32)
    rstd = lax.rsqrt(jnp.mean(token_f * token_f, axis=-1, keepdims=True) + norm_eps)
    normed = (token_f * rstd * norm_gain).astype(jnp.bfloat16)

    picked = expert_ids[:, :, None] == jnp.arange(expert_count, dtype=jnp.int32)[None, None, :]
    weight = jnp.sum(jnp.where(picked, combine_weight[:, :, None], 0.0), axis=1)
    payload = row_major(jnp.concatenate([normed] + three_parts(weight), axis=1))

    lines = [
        [plane * 2 * QUARTERS + place for plane in range(planes)] for place in range(2 * QUARTERS)
    ]

    def gather_column(block):
        return row_major(
            lax.all_gather(block, "sq", axis=0, tiled=True, axis_index_groups=lines)
        )

    column_x = gather_column(payload)

    parts = column_x[:, width:].astype(jnp.float32).reshape(column, 3, expert_count)
    column_weight = parts[:, 0] + parts[:, 1] + parts[:, 2]
    slot_iota = lax.broadcasted_iota(jnp.int32, (slots, column), 0)
    earlier = lax.broadcasted_iota(jnp.int32, (column, column), 0) < lax.broadcasted_iota(
        jnp.int32, (column, column), 1
    )

    def choose(which):
        experts = jnp.arange(expert_count, dtype=jnp.int32)
        mine = jnp.sum(jnp.where(experts[None, :] == which, column_weight, 0.0), axis=1)
        mask = mine > 0.0
        slot = jnp.sum(jnp.where(earlier & mask[:, None], 1, 0), axis=0)
        hit = (slot_iota == slot[None, :]) & mask[None, :]
        row_weight = jnp.sum(jnp.where(hit, mine[None, :], 0.0), axis=1, keepdims=True)
        return hit.astype(jnp.bfloat16), row_weight

    own_select, own_weight = choose(expert)
    far_select, far_weight = choose(expert ^ 1)

    def rows_x(select):
        return jnp.dot(select, column_x[:, :width], preferred_element_type=jnp.float32).astype(
            jnp.bfloat16
        )

    own_x = rows_x(own_select)
    far_x = rows_x(far_select)
    side_x = flip(far_x, SIDE)
    pair_x = flip(own_x, PAIR)
    across_x = flip(far_x, PAIR | SIDE)
    column_cot = behind(gather_column(cotangent), (side_x, pair_x, across_x))

    def rows_dy(select, row_weight):
        rows = jnp.dot(select, column_cot, preferred_element_type=jnp.float32)
        return (rows * row_weight).astype(jnp.bfloat16)

    own_dy = rows_dy(own_select, own_weight)
    far_dy = rows_dy(far_select, far_weight)
    side_dy = flip(far_dy, SIDE)
    pair_dy = flip(own_dy, PAIR)

    def both_cores(first, second):
        rows = jnp.concatenate([first, second], axis=0)
        return jnp.concatenate([rows, flip(rows, CORE)], axis=0)

    gate_w = fast_copy(behind(w_gate[0], (own_dy, far_dy)).T).T
    up_w = w_up[0]

    def forward(x_in):
        gate = jnp.dot(x_in, gate_w, preferred_element_type=jnp.float32)
        up = jnp.dot(x_in, up_w, preferred_element_type=jnp.float32)
        return gate, up

    def hidden(gate, up, dy_e):
        sig = jax.nn.sigmoid(glu_alpha * gate)
        glu = gate * sig
        hid = (glu * (up + 1.0)).astype(jnp.bfloat16)
        d_hid = contract_cols(dy_e, down_w)
        d_up = (d_hid * glu).astype(jnp.bfloat16)
        d_gate = (d_hid * (up + 1.0) * (sig + glu_alpha * gate * sig * (1.0 - sig))).astype(
            jnp.bfloat16
        )
        return hid, d_gate, d_up

    def row_gradient(d_gate, d_up, first, last):
        return (
            contract_cols(d_gate, gate_w[first:last]) + contract_cols(d_up, up_w[first:last])
        ).astype(jnp.bfloat16)

    own_x, side_x, pair_x, across_x = behind((own_x, side_x, pair_x, across_x), (own_dy, far_dy))
    chip_x = both_cores(own_x, side_x)
    pair_x = both_cores(pair_x, across_x)
    chip_forward = forward(chip_x)
    side_dy, pair_dy = behind((side_dy, pair_dy), chip_forward)
    across_dy = flip(side_dy, PAIR)
    down_w = fast_copy(behind(w_down[0], side_dy))
    chip_dy = both_cores(own_dy, side_dy)
    pair_forward = forward(behind(pair_x, chip_dy))
    chip_hid, chip_d_gate, chip_d_up = hidden(*chip_forward, chip_dy)
    chip_rows = row_gradient(chip_d_gate, chip_d_up, 0, width)
    chip_sum = chip_rows[:kept].astype(jnp.float32) + flip(chip_rows[kept:], CORE).astype(
        jnp.float32
    )
    side_ready = chip_sum[slots:].astype(jnp.bfloat16)
    side_sum = flip(side_ready, SIDE)

    pair_core_dy = flip(pair_dy, CORE)
    across_dy = behind(across_dy, (chip_sum, pair_forward))
    pair_dy = jnp.concatenate([pair_dy, across_dy, pair_core_dy, flip(across_dy, CORE)], axis=0)
    pair_hid, pair_d_gate, pair_d_up = hidden(*pair_forward, pair_dy)

    cut = width // 2 // 128 * 128
    spans = [(0, cut), (cut, width)]

    def core_sum(rows, from_core):
        total = rows[:kept].astype(jnp.float32) + from_core.astype(jnp.float32)
        return total.astype(jnp.bfloat16)

    def to_pair(rows):
        return flip(rows[:slots], PAIR), flip(rows[slots:], PAIR | SIDE)

    rows_first = row_gradient(*behind((pair_d_gate, pair_d_up), side_ready), *spans[0])
    core_first = flip(rows_first[kept:], CORE)
    rows_second = row_gradient(*behind((pair_d_gate, pair_d_up), rows_first), *spans[1])
    sum_first = core_sum(rows_first, core_first)
    core_second = flip(behind(rows_second[kept:], sum_first), CORE)
    sent_first = to_pair(sum_first)

    x_in = jnp.concatenate([chip_x, pair_x], axis=0)
    dy_e = jnp.concatenate([chip_dy, pair_dy], axis=0)
    hid = jnp.concatenate([chip_hid, pair_hid], axis=0)
    d_gate = jnp.concatenate([chip_d_gate, pair_d_gate], axis=0)
    d_up = jnp.concatenate([chip_d_up, pair_d_up], axis=0)

    def to_column(span, from_pair, from_across):
        first, last = span
        own_rows = chip_sum[:slots, first:last] + from_pair.astype(jnp.float32)
        far_rows = side_sum[:, first:last].astype(jnp.float32) + from_across.astype(jnp.float32)
        return row_major(
            contract_rows(own_select, own_rows.astype(jnp.bfloat16))
            + contract_rows(far_select, far_rows.astype(jnp.bfloat16))
        )

    def to_tokens(d_column):
        blocks = d_column.reshape(planes, tok_count, d_column.shape[1])
        total = lax.dynamic_index_in_dim(blocks, plane, 0, False)
        got = []
        for s in range(1, planes):
            block = lax.dynamic_index_in_dim(blocks, (plane + s) % planes, 0, False)
            got.append(shift(block.astype(jnp.bfloat16), s))
        return total, got

    def added(total, got):
        for block in got:
            total = total + block.astype(jnp.float32)
        return total

    def weight_gradient(hidden_rows, model_rows, first):
        return weight_product(*behind((hidden_rows, model_rows), first))

    grad_gate = weight_gradient(d_gate, x_in, (sum_first, rows_second, chip_sum))
    sum_second = core_sum(*behind((rows_second, core_second), grad_gate))
    sent_second = to_pair(sum_second)
    d_column = to_column(spans[0], *behind(sent_first, (grad_gate, sum_second)))
    first_half = to_tokens(d_column)
    grad_up = weight_gradient(d_up, x_in, d_column)
    first_half = added(*behind(first_half, grad_up))
    d_column = to_column(spans[1], *behind(sent_second, first_half))
    second_half = to_tokens(d_column)
    grad_down = weight_gradient(hid, dy_e, d_column)
    second_half = added(*behind(second_half, grad_down))
    grads = [grad_gate.T[None], grad_up.T[None], grad_down[None]]
    d_normed = jnp.concatenate([first_half, second_half], axis=1)

    scaled = d_normed * norm_gain
    mixed = jnp.mean(token_f * scaled, axis=-1, keepdims=True)
    d_tokens = (rstd * scaled - token_f * rstd * rstd * rstd * mixed).astype(jnp.bfloat16)
    return (d_tokens, *grads)


def solution(mesh):
    placed = (
        P("sq", None),
        P(),
        P("sq", None),
        P("sq", None),
        P("sq", None),
        P("sq", None, None),
        P("sq", None, None),
        P("sq", None, None),
    )
    return jax.shard_map(
        local,
        mesh=mesh,
        in_specs=placed,
        out_specs=(P("sq", None), P("sq", None, None), P("sq", None, None), P("sq", None, None)),
        check_vma=False,
    )
```
